32 devices in a mesh: ens: 4 (over z), dom: 8 (over y, x, core).
Axes of the slice: x: 2, y: 2, z: 4, core: 2. Of those that a mesh axis runs over, the one named last changes fastest.
Arguments:
- state: float32 [128, 256, 128], P('ens', 'dom'), may hold values from -6 to 6
- row_courant: float32 [256, 128], P('dom'), may hold values from 0.3 to 0.6
- col_courant: float32 [256, 128], P('dom'), may hold values from 0.05 to 0.2
- diffusion: float32 [256, 128], P('dom'), may hold values from 0.01 to 0.05
- obs_values: float32 [4, 256], replicated, may hold values from -8 to 8
- obs_variance: float32 [4, 256], replicated, may hold values from 0.25 to 4
- obs_offsets: int32 [4, 256], replicated, may hold values from 0 to 4095
- owners: int32 [4], replicated, may hold values from 0 to 7, as said below
Outputs:
- analysis: float32 [128, 256, 128], P('ens', 'dom')
The draws below stay inside these ranges and needn't reach their ends.
Inputs may be any that keep to these rules, and one draw needn't show every extreme that they name: `owners`: distinct domain blocks, one for each batch.
All inputs are finite; a program needn't handle non-finite values.
Results may differ from the reference program's by a relative error of at most 0.0002.
Values sent between devices are 32-bit elements; how exact they have to be, the bound alone decides.
No kernel may reach another device: no remote copies, remote signals or barrier semaphores. Data moves between devices by JAX's collectives and lax.ppermute only.
A program may use at most 64 MiB of HBM per device.

```python
import math
import jax
import jax.numpy as jnp
from jax import lax

ROWS_DEV = 32
COLS = 128
NOB = 256
NB = 4
FSTEPS = 4
MEMBERS = 128
ROWS = 256
N_DOM = 8


def draw_owners(key, part):
    inner_key = jax.random.fold_in(key, 11)
    order_key = jax.random.fold_in(key, 23)
    inner = 1 + jax.random.permutation(inner_key, N_DOM - 2)[:NB - 2]
    ends = jnp.array([0, N_DOM - 1], dtype=jnp.int32)
    values = jnp.concatenate([ends, inner.astype(jnp.int32)])
    order = jax.random.permutation(order_key, NB)
    return values[order].astype(jnp.int32)


def touch_ends(values, key, low, largest):
    longest = values.shape.index(max(values.shape))
    spots = []
    for shift in (0, 1):
        where = [jax.random.randint(jax.random.fold_in(key, axis), (), 0, length) for axis, length in enumerate(values.shape)]
        where[longest] = (where[longest] + shift) % values.shape[longest]
        spots.append(tuple(where))
    return values.at[spots[0]].set(low).at[spots[1]].set(largest)


def steps_of(own_key, dims, cuts, low, top_value):
    def one(axis_at, parts):
        steps = jax.random.uniform(jax.random.fold_in(jax.random.fold_in(own_key, 6), axis_at), (parts,), jnp.float32, low / len(cuts), top_value / len(cuts))
        return jnp.repeat(jnp.exp(steps), dims[axis_at] // parts).reshape((-1,) + (1,) * (len(dims) - axis_at - 1))

    loudness = one(*cuts[0])
    for cut in cuts[1:]:
        loudness = loudness * one(*cut)
    return loudness


def centred(rng, shape, scale, most, pieces=(), kind=jnp.bfloat16):
    gain = steps_of(rng, shape, pieces, -0.22, 0.18) if pieces else 1.0
    drawn = jax.random.normal(rng, shape, jnp.float32) * scale * gain
    return jnp.minimum(jnp.maximum(drawn, -most), most).astype(kind)


def setup_inputs(seed: int = 0) -> dict:
    splits = jax.random.split(jax.random.key(seed), 9)
    return {
        "state": centred(splits[0], (MEMBERS, ROWS, COLS), 1.0, 6.0, ((0, 4), (1, 8)), jnp.float32),
        "row_courant": jnp.clip(0.3 + 0.3 * jax.random.uniform(splits[1], (ROWS, COLS), jnp.float32) ** steps_of(splits[1], (ROWS, COLS), ((0, 8),), -0.2, 0.2), 0.3, 0.6),
        "col_courant": jnp.clip(0.05 + 0.15 * jax.random.uniform(splits[2], (ROWS, COLS), jnp.float32) ** steps_of(splits[2], (ROWS, COLS), ((0, 8),), -0.2, 0.2), 0.05, 0.2),
        "diffusion": jnp.clip(0.01 + 0.04 * jax.random.uniform(splits[3], (ROWS, COLS), jnp.float32) ** steps_of(splits[3], (ROWS, COLS), ((0, 8),), -0.2, 0.2), 0.01, 0.05),
        "obs_values": centred(splits[4], (NB, NOB), 1.5, 8.0, (), jnp.float32),
        "obs_variance": jnp.clip(jnp.exp(jax.random.uniform(splits[5], (NB, NOB), jnp.float32, math.log(0.25), math.log(4.0))), 0.25, 4.0),
        "obs_offsets": touch_ends(jax.random.randint(splits[6], (NB, NOB), 0, ROWS_DEV * COLS), jax.random.fold_in(splits[6], 1), 0, (ROWS_DEV * COLS) - 1).astype(jnp.int32),
        "owners": draw_owners(jax.random.fold_in(splits[8], 71), 0),
    }


def advance(field, row_courant, col_courant, diffusion):
    upper = jnp.roll(field, 1, axis=1)
    lower = jnp.roll(field, -1, axis=1)
    left = jnp.roll(field, 1, axis=2)
    right = jnp.roll(field, -1, axis=2)
    return field - row_courant * (field - upper) - col_courant * (field - left) + diffusion * (upper + lower + left + right - 4.0 * field)

def reference(state, row_courant, col_courant, diffusion, obs_values, obs_variance, obs_offsets, owners):
    field = state
    for step in range(FSTEPS):
        field = advance(field, row_courant, col_courant, diffusion)
    members = field.shape[0]
    matrix = field.reshape(members, ROWS * COLS)
    for batch in range(NB):
        cells = (owners[batch] * (ROWS_DEV * COLS) + obs_offsets[batch]).astype(jnp.int32)
        observed = jnp.take(matrix, cells, axis=1)
        ybar = jnp.mean(observed, axis=0)
        anom_obs = observed - ybar
        system = jnp.dot(anom_obs.T, anom_obs, precision=lax.Precision.HIGHEST) / (members - 1.0)
        system = system + jnp.diag(obs_variance[batch])
        factor = jnp.linalg.cholesky(system)
        target = (obs_values[batch] - ybar)[None, :] - 0.5 * anom_obs
        weights = jax.scipy.linalg.cho_solve((factor, True), target.T).T
        anomaly = matrix - jnp.mean(matrix, axis=0)
        spread = jnp.dot(anom_obs.T, anomaly, precision=lax.Precision.HIGHEST) / (members - 1.0)
        matrix = matrix + jnp.dot(weights, spread, precision=lax.Precision.HIGHEST)
    return matrix.reshape(state.shape)
```

```python
import functools

import jax
import jax.numpy as jnp
from jax import lax
from jax.experimental import pallas as pl
from jax.experimental.pallas import tpu as pltpu
from jax.sharding import PartitionSpec as P

FSTEPS = 4
TOLERANCE = 1e-6
WIDE_BOUND = 16.0
HIGHEST = lax.Precision.HIGHEST
NN = (((1,), (0,)), ((), ()))
NT = (((1,), (1,)), ((), ()))

VMEM = pl.BlockSpec(memory_space=pltpu.VMEM)
SMEM = pl.BlockSpec(memory_space=pltpu.SMEM)
PARAMS = pltpu.CompilerParams(vmem_limit_bytes=40 * 1024 * 1024)


def own_batch(place_ref, owners_ref):
    batch = jnp.int32(0)
    for i in range(owners_ref.shape[0]):
        batch = jnp.where(owners_ref[i] == place_ref[0], i, batch)
    return batch


def forecast_kernel(
    place_ref, owners_ref, offsets_ref, state_ref, row_ref, col_ref, diff_ref, up_ref, down_ref,
    field_ref, seen_ref, a_ref, b_ref, coef_ref,
):
    rows, mem, cols = field_ref.shape
    width = FSTEPS
    span = rows + 2 * width
    for r in range(width):
        a_ref[r] = up_ref[r, :mem, :]
        a_ref[width + rows + r] = down_ref[r, :mem, :]

    @pl.loop(0, rows, unroll=4)
    def _(r):
        a_ref[width + r] = state_ref[pl.ds(r, mem, stride=rows), :]

    def put_coefs(r, row_c, col_c, diff_c):
        shape = (8, cols)
        coef_ref[0, r] = jnp.broadcast_to(1.0 - row_c - col_c - 4.0 * diff_c, shape)
        coef_ref[1, r] = jnp.broadcast_to(row_c + diff_c, shape)
        coef_ref[2, r] = jnp.broadcast_to(col_c + diff_c, shape)
        coef_ref[3, r] = jnp.broadcast_to(diff_c, shape)

    for r in range(width):
        for base, ref in ((r, up_ref), (width + rows + r, down_ref)):
            put_coefs(base, *[ref[r, mem + i:mem + i + 1, :] for i in range(3)])
    for r in range(rows):
        put_coefs(width + r, row_ref[r:r + 1, :], col_ref[r:r + 1, :], diff_ref[r:r + 1, :])

    source, target = a_ref, b_ref
    for step in range(1, FSTEPS + 1):
        last = step == FSTEPS

        def one_row(r, source=source, target=target, last=last):
            x = source[r]
            left = pltpu.roll(x, 1, 1)
            right = pltpu.roll(x, cols - 1, 1)
            fold = lambda v: v.reshape(mem // 8, 8, cols)
            fresh = (
                coef_ref[0, r][None] * fold(x)
                + coef_ref[1, r][None] * fold(source[r - 1])
                + coef_ref[2, r][None] * fold(left)
                + coef_ref[3, r][None] * (fold(source[r + 1]) + fold(right))
            ).reshape(mem, cols)
            if last:
                field_ref[r - width] = fresh
            else:
                target[r] = fresh

        pl.loop(step, span - step, unroll=2)(one_row)
        source, target = target, source

    batch = own_batch(place_ref, owners_ref)
    lanes = lax.broadcasted_iota(jnp.int32, (mem, cols), 1)
    for part in range(seen_ref.shape[1] // cols):

        def pick(k, total, part=part):
            cell = offsets_ref[batch, part * cols + k]
            row = cell // cols
            lane = cell - row * cols
            moved = pltpu.roll(field_ref[row], lax.rem(k - lane + cols, cols), 1)
            return jnp.where(lanes == k, moved, total)

        total = lax.fori_loop(0, cols, pick, jnp.zeros((mem, cols), jnp.float32), unroll=8)
        seen_ref[:, part * cols:(part + 1) * cols] = total


def gram_kernel(place_ref, owners_ref, obs_ref, var_ref, *refs):
    seen_refs, out_ref = refs[:-1], refs[-1]
    batch = own_batch(place_ref, owners_ref)
    seen = jnp.concatenate([ref[...] for ref in seen_refs], axis=0)
    members, count = seen.shape
    ybar = jnp.mean(seen, axis=0, keepdims=True)
    anom = seen - ybar
    weight = 1.0 / (var_ref[pl.ds(batch, 1), :] * (members - 1.0))
    gap = obs_ref[pl.ds(batch, 1), :] - ybar
    left = jnp.concatenate([anom * weight, jnp.broadcast_to(gap * weight, (8, count))], axis=0)
    out_ref[...] = lax.dot_general(
        left, anom, NT, precision=HIGHEST, preferred_element_type=jnp.float32
    )


def split(x):
    high = x.astype(jnp.bfloat16)
    return high, (x - high.astype(jnp.float32)).astype(jnp.bfloat16)


def product(wide, a, b, dims=NN):
    dot = functools.partial(
        lax.dot_general, dimension_numbers=dims, preferred_element_type=jnp.float32
    )
    if wide:
        return dot(a, b, precision=HIGHEST)
    a_high, a_low = split(a)
    b_high, b_low = split(b)
    return dot(a_high, b_high) + (dot(a_high, b_low) + dot(a_low, b_high))


def chain_kernel(owners_ref, gram_ref, out_ref):
    mem, members = out_ref.shape
    batches = owners_ref.shape[0]
    eye = (
        lax.broadcasted_iota(jnp.int32, (members, members), 0)
        == lax.broadcasted_iota(jnp.int32, (members, members), 1)
    ).astype(jnp.float32)

    def chain(wide):
        mul = functools.partial(product, wide)
        trans = mean_row = forward = None
        for b in range(batches):
            gram = gram_ref[owners_ref[b], :members, :]
            lead = gram_ref[owners_ref[b], members:members + 8, :]
            if b == 0:
                excess, vec = gram, lead
                trans, mean_row = eye, jnp.zeros_like(lead)
            else:
                first = mul(jnp.concatenate([gram, lead], axis=0), trans)
                second = mul(jnp.concatenate([forward, mean_row], axis=0), first[:members])
                excess = second[:members]
                vec = first[members:] - second[members:]
            bound = 1.0 + jnp.max(jnp.sum(jnp.abs(excess), axis=0, keepdims=True))
            scale = 2.0 / (1.0 + bound)
            off = (bound - 1.0) / (bound + 1.0)
            rest = (1.0 - scale) * eye - scale * excess
            power = scale * jnp.concatenate([trans, vec], axis=0)

            def unfinished(carry):
                off = carry[0]
                return off * off / (2.0 - off * off) > TOLERANCE

            def refine(carry):
                off, rest, power = carry
                factor = 2.0 / (2.0 - off * off)
                both = mul(jnp.concatenate([rest, power], axis=0), rest)
                rest = factor * both[:members] + (1.0 - factor) * eye
                power = factor * (power + both[members:])
                return off * off / (2.0 - off * off), rest, power

            off, rest, power = lax.while_loop(unfinished, refine, (off, rest, power))
            power = 2.0 / (2.0 - off * off) * (power + mul(power, rest))
            move = power[members:]
            mean_row = mean_row + (move if b == 0 else mul(move, forward))
            trans = 0.5 * (trans + power[:members])
            forward = trans.T
        out_ref[...] = forward[:mem] + mean_row[:1]

    worst = jnp.float32(0.0)
    for b in range(batches):
        gram = gram_ref[owners_ref[b], :members, :]
        worst = jnp.maximum(worst, jnp.max(jnp.sum(jnp.abs(gram), axis=0, keepdims=True)))
    pl.when(worst > WIDE_BOUND)(lambda: chain(True))
    pl.when(jnp.logical_not(worst > WIDE_BOUND))(lambda: chain(False))


def apply_kernel(mix_ref, *refs):
    field_refs, out_ref = refs[:-1], refs[-1]
    rows, mem, cols = field_refs[0].shape
    mix_high, mix_low = split(mix_ref[...])
    dot = functools.partial(jnp.dot, preferred_element_type=jnp.float32)

    @pl.loop(0, rows // 2, unroll=2)
    def _(pair):
        r = 2 * pair
        x = jnp.concatenate(
            [jnp.concatenate([ref[r + i] for ref in field_refs], axis=0) for i in range(2)], axis=1
        )
        high, low = split(x)
        fresh = dot(mix_high, high) + (dot(mix_high, low) + dot(mix_low, high))
        for i in range(2):
            out_ref[pl.ds(r + i, mem, stride=rows), :] = fresh[:, i * cols:(i + 1) * cols]


def shift(x, axis, step):
    count = lax.axis_size(axis)
    return lax.ppermute(x, axis, [(i, (i + step) % count) for i in range(count)])


def on_device(
    state, row_courant, col_courant, diffusion, obs_values, obs_variance, obs_offsets, owners
):
    mem, rows, cols = state.shape
    ens = lax.axis_size("ens")
    members = mem * ens
    observed = obs_values.shape[1]
    f32 = functools.partial(jax.ShapeDtypeStruct, dtype=jnp.float32)
    place = lax.axis_index("dom").astype(jnp.int32).reshape(1)

    def edge(part):
        coefs = jnp.stack([row_courant[part], col_courant[part], diffusion[part]], axis=1)
        return jnp.concatenate([state[:, part].transpose(1, 0, 2), coefs], axis=1)

    up = shift(edge(slice(rows - FSTEPS, rows)), "dom", 1)
    down = shift(edge(slice(0, FSTEPS)), "dom", -1)
    span = rows + 2 * FSTEPS
    field, seen = pl.pallas_call(
        forecast_kernel,
        out_shape=(f32((rows, mem, cols)), f32((mem, observed))),
        in_specs=[SMEM] * 3 + [VMEM] * 6,
        out_specs=(VMEM, VMEM),
        scratch_shapes=[
            pltpu.VMEM((span, mem, cols), jnp.float32),
            pltpu.VMEM((span, mem, cols), jnp.float32),
            pltpu.VMEM((4, span, 8, cols), jnp.float32),
        ],
        compiler_params=PARAMS,
        name="forecast",
    )(place, owners, obs_offsets, state.reshape(mem * rows, cols), row_courant, col_courant,
      diffusion, up, down)

    seens = [seen] + [shift(seen, "ens", k) for k in range(1, ens)]
    gram = pl.pallas_call(
        gram_kernel,
        out_shape=f32((members + 8, members)),
        in_specs=[SMEM] * 2 + [VMEM] * (2 + ens),
        out_specs=VMEM,
        compiler_params=PARAMS,
        name="gram",
    )(place, owners, obs_values, obs_variance, *seens)
    grams = lax.all_gather(gram, "dom")

    fields = [field]
    for _ in range(1, ens):
        fields.append(shift(fields[-1], "ens", 1))

    mix = pl.pallas_call(
        chain_kernel,
        out_shape=f32((mem, members)),
        in_specs=[SMEM, VMEM],
        out_specs=VMEM,
        compiler_params=PARAMS,
        cost_estimate=pl.CostEstimate(
            flops=2 * 4 * 20 * members**3, bytes_accessed=grams.size * 4, transcendentals=0
        ),
        name="chain",
    )(owners, grams)
    out = pl.pallas_call(
        apply_kernel,
        out_shape=f32((mem * rows, cols)),
        in_specs=[VMEM] * (1 + ens),
        out_specs=VMEM,
        compiler_params=PARAMS,
        name="apply",
    )(mix, *fields)
    return out.reshape(mem, rows, cols)


def solution(mesh):
    return jax.shard_map(
        on_device,
        mesh=mesh,
        in_specs=(
            P("ens", "dom", None),
            P("dom", None),
            P("dom", None),
            P("dom", None),
            P(),
            P(),
            P(),
            P(),
        ),
        out_specs=P("ens", "dom", None),
        check_vma=False,
    )
```

```python
import functools

import jax
import jax.numpy as jnp
from jax import lax
from jax.experimental import pallas as pl
from jax.experimental.pallas import tpu as pltpu
from jax.sharding import PartitionSpec as P

FSTEPS = 4
TOLERANCE = 1e-6
WIDE_BOUND = 16.0
HIGHEST = lax.Precision.HIGHEST
NN = (((1,), (0,)), ((), ()))
NT = (((1,), (1,)), ((), ()))

VMEM = pl.BlockSpec(memory_space=pltpu.VMEM)
SMEM = pl.BlockSpec(memory_space=pltpu.SMEM)
PARAMS = pltpu.CompilerParams(vmem_limit_bytes=40 * 1024 * 1024)


def own_batch(place_ref, owners_ref):
    batch = jnp.int32(0)
    for i in range(owners_ref.shape[0]):
        batch = jnp.where(owners_ref[i] == place_ref[0], i, batch)
    return batch


def estimate(micros):
    return pl.CostEstimate(flops=int(1.15e9 * micros), bytes_accessed=0, transcendentals=0)


def edge_kernel(state_ref, row_ref, col_ref, diff_ref, top_ref, bottom_ref):
    width, _, cols = top_ref.shape
    rows = row_ref.shape[0]
    mem = state_ref.shape[0] // rows
    for r in range(width):
        for ref, row in ((top_ref, r), (bottom_ref, rows - width + r)):
            ref[r, :mem, :] = state_ref[pl.ds(row, mem, stride=rows), :]
            for i, coef in enumerate((row_ref, col_ref, diff_ref)):
                ref[r, mem + i:mem + i + 1, :] = coef[row:row + 1, :]
            ref[r, mem + 3:, :] = jnp.zeros((ref.shape[1] - mem - 3, cols), jnp.float32)


def mixers(row_c, col_c, diff_c):
    return 1.0 - row_c - col_c - 4.0 * diff_c, row_c + diff_c, col_c + diff_c, diff_c


def advance(load, coef, store, count, scratches):
    for step in range(1, FSTEPS + 1):
        source = load if step == 1 else scratches[step % 2].__getitem__
        for r in range(step, count - step):
            x = source(r)
            cols = x.shape[1]
            here, upper, side, lower = coef(r)
            fresh = (
                here * x
                + upper * source(r - 1)
                + side * pltpu.roll(x, 1, 1)
                + lower * (source(r + 1) + pltpu.roll(x, cols - 1, 1))
            )
            if step == FSTEPS:
                store(r, fresh)
            else:
                scratches[(step + 1) % 2][r] = fresh


def inner_kernel(state_ref, row_ref, col_ref, diff_ref, inner_ref, a_ref, b_ref):
    rows = row_ref.shape[0]
    mem = state_ref.shape[0] // rows

    def load(r):
        return state_ref[pl.ds(r, mem, stride=rows), :]

    def coef(r):
        return mixers(row_ref[r:r + 1, :], col_ref[r:r + 1, :], diff_ref[r:r + 1, :])

    def store(r, value):
        inner_ref[r - FSTEPS] = value

    advance(load, coef, store, rows, (a_ref, b_ref))


def outer_kernel(
    place_ref, owners_ref, offsets_ref, state_ref, row_ref, col_ref, diff_ref, up_ref, down_ref,
    inner_ref, outer_ref, seen_ref, a_ref, b_ref, field_ref,
):
    width = FSTEPS
    rows, mem, cols = field_ref.shape

    for side in range(2):
        base = rows - 2 * width if side else -width

        def place(r, side=side):
            row = r + (rows - 2 * width if side else -width)
            if row < 0:
                return up_ref, row + width
            if row >= rows:
                return down_ref, row - rows
            return None, row

        def load(r, place=place):
            ref, row = place(r)
            return state_ref[pl.ds(row, mem, stride=rows), :] if ref is None else ref[row, :mem, :]

        def coef(r, place=place):
            ref, row = place(r)
            if ref is None:
                return mixers(*[c[row:row + 1, :] for c in (row_ref, col_ref, diff_ref)])
            return mixers(*[ref[row, mem + i:mem + i + 1, :] for i in range(3)])

        def store(r, value, side=side, base=base):
            outer_ref[side * width + r - width] = value
            field_ref[r + base] = value

        advance(load, coef, store, 3 * width, (a_ref, b_ref))

    for r in range(rows - 2 * width):
        field_ref[width + r] = inner_ref[r]

    batch = own_batch(place_ref, owners_ref)
    lanes = lax.broadcasted_iota(jnp.int32, (mem, cols), 1)
    for part in range(seen_ref.shape[1] // cols):

        def pick(k, total, part=part):
            cell = offsets_ref[batch, part * cols + k]
            row = cell // cols
            lane = cell - row * cols
            moved = pltpu.roll(field_ref[row], lax.rem(k - lane + cols, cols), 1)
            return jnp.where(lanes == k, moved, total)

        total = lax.fori_loop(0, cols, pick, jnp.zeros((mem, cols), jnp.float32), unroll=32)
        seen_ref[:, part * cols:(part + 1) * cols] = total


def gram_kernel(place_ref, owners_ref, obs_ref, var_ref, *refs):
    seen_refs, out_ref = refs[:-1], refs[-1]
    batch = own_batch(place_ref, owners_ref)
    seen = jnp.concatenate([ref[...] for ref in seen_refs], axis=0)
    members, count = seen.shape
    ybar = jnp.mean(seen, axis=0, keepdims=True)
    anom = seen - ybar
    weight = 1.0 / (var_ref[pl.ds(batch, 1), :] * (members - 1.0))
    gap = obs_ref[pl.ds(batch, 1), :] - ybar
    left = jnp.concatenate([anom * weight, jnp.broadcast_to(gap * weight, (8, count))], axis=0)
    out_ref[...] = lax.dot_general(
        left, anom, NT, precision=HIGHEST, preferred_element_type=jnp.float32
    )


def split(x):
    high = x.astype(jnp.bfloat16)
    return high, (x - high.astype(jnp.float32)).astype(jnp.bfloat16)


def product(wide, a, b, dims=NN):
    dot = functools.partial(
        lax.dot_general, dimension_numbers=dims, preferred_element_type=jnp.float32
    )
    if wide:
        return dot(a, b, precision=HIGHEST)
    a_high, a_low = split(a)
    b_high, b_low = split(b)
    return dot(a_high, b_high) + (dot(a_high, b_low) + dot(a_low, b_high))


def chain_kernel(owners_ref, gram_ref, out_ref):
    mem, members = out_ref.shape
    batches = owners_ref.shape[0]
    eye = (
        lax.broadcasted_iota(jnp.int32, (members, members), 0)
        == lax.broadcasted_iota(jnp.int32, (members, members), 1)
    ).astype(jnp.float32)

    def chain(wide):
        mul = functools.partial(product, wide)
        trans = mean_row = forward = None
        for b in range(batches):
            gram = gram_ref[owners_ref[b], :members, :]
            lead = gram_ref[owners_ref[b], members:members + 8, :]
            if b == 0:
                excess, vec = gram, lead
                trans, mean_row = eye, jnp.zeros_like(lead)
            else:
                first = mul(jnp.concatenate([gram, lead], axis=0), trans)
                second = mul(jnp.concatenate([forward, mean_row], axis=0), first[:members])
                excess = second[:members]
                vec = first[members:] - second[members:]
            bound = 1.0 + jnp.max(jnp.sum(jnp.abs(excess), axis=0, keepdims=True))
            scale = 2.0 / (1.0 + bound)
            off = (bound - 1.0) / (bound + 1.0)
            rest = (1.0 - scale) * eye - scale * excess
            power = scale * jnp.concatenate([trans, vec], axis=0)

            def unfinished(carry):
                off = carry[0]
                return off * off / (2.0 - off * off) > TOLERANCE

            def refine(carry):
                off, rest, power = carry
                factor = 2.0 / (2.0 - off * off)
                both = mul(jnp.concatenate([rest, power], axis=0), rest)
                rest = factor * both[:members] + (1.0 - factor) * eye
                power = factor * (power + both[members:])
                return off * off / (2.0 - off * off), rest, power

            off, rest, power = lax.while_loop(unfinished, refine, (off, rest, power))
            power = 2.0 / (2.0 - off * off) * (power + mul(power, rest))
            move = power[members:]
            mean_row = mean_row + (move if b == 0 else mul(move, forward))
            trans = 0.5 * (trans + power[:members])
            forward = trans.T
        out_ref[...] = forward[:mem] + mean_row[:1]

    worst = jnp.float32(0.0)
    for b in range(batches):
        gram = gram_ref[owners_ref[b], :members, :]
        worst = jnp.maximum(worst, jnp.max(jnp.sum(jnp.abs(gram), axis=0, keepdims=True)))
    pl.when(worst > WIDE_BOUND)(lambda: chain(True))
    pl.when(jnp.logical_not(worst > WIDE_BOUND))(lambda: chain(False))


def apply_kernel(mix_ref, *refs):
    field_refs, out_ref = refs[:-1], refs[-1]
    inner_refs, outer_refs = field_refs[::2], field_refs[1::2]
    inner, mem, cols = inner_refs[0].shape
    outer = outer_refs[0].shape[0]
    rows, width = inner + outer, outer // 2
    mix_high, mix_low = split(mix_ref[...])
    dot = functools.partial(jnp.dot, preferred_element_type=jnp.float32)

    def part(r):
        if width <= r < rows - width:
            return jnp.concatenate([ref[r - width] for ref in inner_refs], axis=0)
        return jnp.concatenate([ref[r if r < width else r - inner] for ref in outer_refs], axis=0)

    for r in range(0, rows, 2):
        high, low = split(jnp.concatenate([part(r), part(r + 1)], axis=1))
        fresh = dot(mix_high, high) + (dot(mix_high, low) + dot(mix_low, high))
        for i in range(2):
            out_ref[pl.ds(r + i, mem, stride=rows), :] = fresh[:, i * cols:(i + 1) * cols]


def shift(x, axis, step):
    count = lax.axis_size(axis)
    return lax.ppermute(x, axis, [(i, (i + step) % count) for i in range(count)])


def on_device(
    state, row_courant, col_courant, diffusion, obs_values, obs_variance, obs_offsets, owners
):
    mem, rows, cols = state.shape
    ens = lax.axis_size("ens")
    members = mem * ens
    observed = obs_values.shape[1]
    width = FSTEPS
    f32 = functools.partial(jax.ShapeDtypeStruct, dtype=jnp.float32)
    scratch = functools.partial(pltpu.VMEM, dtype=jnp.float32)
    place = lax.axis_index("dom").astype(jnp.int32).reshape(1)
    state = state.reshape(mem * rows, cols)
    coefs = (row_courant, col_courant, diffusion)

    top, bottom = pl.pallas_call(
        edge_kernel,
        out_shape=(f32((width, mem + 8, cols)),) * 2,
        in_specs=[VMEM] * 4,
        out_specs=(VMEM, VMEM),
        compiler_params=PARAMS,
        cost_estimate=estimate(0.5),
        name="edges",
    )(state, *coefs)
    up = shift(bottom, "dom", 1)
    down = shift(top, "dom", -1)
    inner = pl.pallas_call(
        inner_kernel,
        out_shape=f32((rows - 2 * width, mem, cols)),
        in_specs=[VMEM] * 4,
        out_specs=VMEM,
        scratch_shapes=[scratch((rows, mem, cols))] * 2,
        compiler_params=PARAMS,
        cost_estimate=estimate(2),
        name="inner",
    )(state, *coefs)
    outer, seen = pl.pallas_call(
        outer_kernel,
        out_shape=(f32((2 * width, mem, cols)), f32((mem, observed))),
        in_specs=[SMEM] * 3 + [VMEM] * 7,
        out_specs=(VMEM, VMEM),
        scratch_shapes=[scratch((3 * width, mem, cols))] * 2 + [scratch((rows, mem, cols))],
        compiler_params=PARAMS,
        cost_estimate=estimate(3),
        name="outer",
    )(place, owners, obs_offsets, state, *coefs, up, down, inner)

    seens = [seen] + [shift(seen, "ens", k) for k in range(1, ens)]
    gram = pl.pallas_call(
        gram_kernel,
        out_shape=f32((members + 8, members)),
        in_specs=[SMEM] * 2 + [VMEM] * (2 + ens),
        out_specs=VMEM,
        compiler_params=PARAMS,
        cost_estimate=estimate(1),
        name="gram",
    )(place, owners, obs_values, obs_variance, *seens)
    grams = lax.all_gather(gram, "dom")

    def around(part):
        slots = [part] * ens
        for j in range(1, ens // 2 + 1):
            slots[j] = shift(slots[j - 1], "ens", 1)
        for j in range(1, (ens - 1) // 2 + 1):
            slots[ens - j] = shift(slots[(ens - j + 1) % ens], "ens", -1)
        return slots

    fields = [x for pair in zip(around(inner), around(outer)) for x in pair]

    mix = pl.pallas_call(
        chain_kernel,
        out_shape=f32((mem, members)),
        in_specs=[SMEM, VMEM],
        out_specs=VMEM,
        compiler_params=PARAMS,
        cost_estimate=estimate(8),
        name="chain",
    )(owners, grams)
    out = pl.pallas_call(
        apply_kernel,
        out_shape=f32((mem * rows, cols)),
        in_specs=[VMEM] * (1 + 2 * ens),
        out_specs=VMEM,
        compiler_params=PARAMS,
        cost_estimate=estimate(2),
        name="apply",
    )(mix, *fields)
    return out.reshape(mem, rows, cols)


def solution(mesh):
    return jax.shard_map(
        on_device,
        mesh=mesh,
        in_specs=(
            P("ens", "dom", None),
            P("dom", None),
            P("dom", None),
            P("dom", None),
            P(),
            P(),
            P(),
            P(),
        ),
        out_specs=P("ens", "dom", None),
        check_vma=False,
    )
```

```python
import functools

import jax
import jax.numpy as jnp
from jax import lax
from jax.experimental import pallas as pl
from jax.experimental.pallas import tpu as pltpu
from jax.sharding import PartitionSpec as P

FSTEPS = 4
TOLERANCE = 1e-6
WIDE_BOUND = 16.0
CHAIN_US = 2
HIGHEST = lax.Precision.HIGHEST
NN = (((1,), (0,)), ((), ()))
NT = (((1,), (1,)), ((), ()))

VMEM = pl.BlockSpec(memory_space=pltpu.VMEM)
SMEM = pl.BlockSpec(memory_space=pltpu.SMEM)
PARAMS = pltpu.CompilerParams(vmem_limit_bytes=40 * 1024 * 1024)


def own_batch(place_ref, owners_ref):
    batch = jnp.int32(0)
    for i in range(owners_ref.shape[0]):
        batch = jnp.where(owners_ref[i] == place_ref[0], i, batch)
    return batch


def estimate(micros):
    return pl.CostEstimate(flops=int(1.15e9 * micros), bytes_accessed=0, transcendentals=0)


def advance(load, coef, store, count, scratches):
    for step in range(1, FSTEPS + 1):
        source = load if step == 1 else scratches[step % 2].__getitem__
        for r in range(step, count - step):
            x = source(r)
            cols = x.shape[1]
            here, upper, side, lower = coef(r)
            fresh = (
                here * x
                + upper * source(r - 1)
                + side * pltpu.roll(x, 1, 1)
                + lower * (source(r + 1) + pltpu.roll(x, cols - 1, 1))
            )
            if step == FSTEPS:
                store(r, fresh)
            else:
                scratches[(step + 1) % 2][r] = fresh


def inner_kernel(
    state_ref, coef_ref, top_ref, upper_ref, lower_ref, bottom_ref, inner_ref, a_ref, b_ref
):
    width = FSTEPS
    count, rows, cols = coef_ref.shape
    mem = state_ref.shape[0] // rows

    def load(r):
        return state_ref[pl.ds(r, mem, stride=rows), :]

    blocks = (top_ref, 0), (upper_ref, width), (lower_ref, rows - 2 * width), (bottom_ref, rows - width)
    for ref, base in blocks:
        for r in range(width):
            ref[r, :mem, :] = load(base + r)
            for i in range(count):
                ref[r, mem + i:mem + i + 1, :] = coef_ref[i, base + r:base + r + 1, :]
            ref[r, mem + count:, :] = jnp.zeros((ref.shape[1] - mem - count, cols), jnp.float32)

    def coef(r):
        return [coef_ref[i, r:r + 1, :] for i in range(count)]

    def store(r, value):
        inner_ref[r - width] = value

    advance(load, coef, store, rows, (a_ref, b_ref))


def split3(x):
    high, rest = x.astype(jnp.bfloat16), x
    rest = rest - high.astype(jnp.float32)
    middle = rest.astype(jnp.bfloat16)
    return high, middle, (rest - middle.astype(jnp.float32)).astype(jnp.bfloat16)


def outer_kernel(
    place_ref, owners_ref, offsets_ref, up_ref, top_ref, upper_ref, lower_ref, bottom_ref, down_ref,
    inner_ref, outer_ref, seen_ref, a_ref, b_ref,
):
    width = FSTEPS
    inner, mem, cols = inner_ref.shape
    rows = inner + 2 * width
    observed = seen_ref.shape[1]

    for side, refs in enumerate(((up_ref, top_ref, upper_ref), (lower_ref, bottom_ref, down_ref))):

        def load(r, refs=refs):
            return refs[r // width][r % width, :mem, :]

        def coef(r, refs=refs):
            return [refs[r // width][r % width, mem + i:mem + i + 1, :] for i in range(4)]

        def store(r, value, side=side):
            outer_ref[side * width + r - width] = value

        advance(load, coef, store, 3 * width, (a_ref, b_ref))

    def field(r):
        if width <= r < rows - width:
            return inner_ref[r - width]
        return outer_ref[r if r < width else r - inner]

    cells = offsets_ref[pl.ds(own_batch(place_ref, owners_ref), 1), :]
    index = lax.broadcasted_iota(jnp.int32, (2 * cols, observed), 0)
    total = jnp.zeros((3 * mem, observed), jnp.float32)
    for r in range(0, rows, 2):
        parts = jnp.concatenate(split3(jnp.concatenate([field(r), field(r + 1)], axis=1)), axis=0)
        chosen = (index == cells - r * cols).astype(jnp.float32).astype(jnp.bfloat16)
        total = total + jnp.dot(parts, chosen, preferred_element_type=jnp.float32)
    seen_ref[...] = total[:mem] + total[mem:2 * mem] + total[2 * mem:]


def gram_kernel(place_ref, owners_ref, obs_ref, var_ref, *refs):
    seen_refs, out_ref = refs[:-1], refs[-1]
    batch = own_batch(place_ref, owners_ref)
    seen = jnp.concatenate([ref[...] for ref in seen_refs], axis=0)
    members, count = seen.shape
    ybar = jnp.mean(seen, axis=0, keepdims=True)
    anom = seen - ybar
    weight = 1.0 / (var_ref[pl.ds(batch, 1), :] * (members - 1.0))
    gap = obs_ref[pl.ds(batch, 1), :] - ybar
    left = jnp.concatenate([anom * weight, jnp.broadcast_to(gap * weight, (8, count))], axis=0)
    out_ref[...] = lax.dot_general(
        left, anom, NT, precision=HIGHEST, preferred_element_type=jnp.float32
    )


def split(x):
    high = x.astype(jnp.bfloat16)
    return high, (x - high.astype(jnp.float32)).astype(jnp.bfloat16)


def product(wide, a, b, dims=NN):
    dot = functools.partial(
        lax.dot_general, dimension_numbers=dims, preferred_element_type=jnp.float32
    )
    if wide:
        return dot(a, b, precision=HIGHEST)
    a_high, a_low = split(a)
    b_high, b_low = split(b)
    return dot(a_high, b_high) + (dot(a_high, b_low) + dot(a_low, b_high))


def chain_kernel(owners_ref, gram_ref, out_ref):
    mem, members = out_ref.shape
    batches = owners_ref.shape[0]
    eye = (
        lax.broadcasted_iota(jnp.int32, (members, members), 0)
        == lax.broadcasted_iota(jnp.int32, (members, members), 1)
    ).astype(jnp.float32)

    def chain(wide):
        mul = functools.partial(product, wide)
        trans = mean_row = forward = None
        for b in range(batches):
            gram = gram_ref[owners_ref[b], :members, :]
            lead = gram_ref[owners_ref[b], members:members + 8, :]
            if b == 0:
                excess, vec = gram, lead
                trans, mean_row = eye, jnp.zeros_like(lead)
            else:
                first = mul(jnp.concatenate([gram, lead], axis=0), trans)
                second = mul(jnp.concatenate([forward, mean_row], axis=0), first[:members])
                excess = second[:members]
                vec = first[members:] - second[members:]
            bound = 1.0 + jnp.max(jnp.sum(jnp.abs(excess), axis=0, keepdims=True))
            scale = 2.0 / (1.0 + bound)
            off = (bound - 1.0) / (bound + 1.0)
            rest = (1.0 - scale) * eye - scale * excess
            power = scale * jnp.concatenate([trans, vec], axis=0)

            def unfinished(carry):
                off = carry[0]
                return off * off / (2.0 - off * off) > TOLERANCE

            def refine(carry):
                off, rest, power = carry
                factor = 2.0 / (2.0 - off * off)
                both = mul(jnp.concatenate([rest, power], axis=0), rest)
                rest = factor * both[:members] + (1.0 - factor) * eye
                power = factor * (power + both[members:])
                return off * off / (2.0 - off * off), rest, power

            off, rest, power = lax.while_loop(unfinished, refine, (off, rest, power))
            power = 2.0 / (2.0 - off * off) * (power + mul(power, rest))
            move = power[members:]
            mean_row = mean_row + (move if b == 0 else mul(move, forward))
            trans = 0.5 * (trans + power[:members])
            forward = trans.T
        out_ref[...] = forward[:mem] + mean_row[:1]

    worst = jnp.float32(0.0)
    for b in range(batches):
        gram = gram_ref[owners_ref[b], :members, :]
        worst = jnp.maximum(worst, jnp.max(jnp.sum(jnp.abs(gram), axis=0, keepdims=True)))
    pl.when(worst > WIDE_BOUND)(lambda: chain(True))
    pl.when(jnp.logical_not(worst > WIDE_BOUND))(lambda: chain(False))


def apply_kernel(mix_ref, *refs):
    field_refs, out_ref = refs[:-1], refs[-1]
    inner_refs, outer_refs = field_refs[::2], field_refs[1::2]
    inner, mem, cols = inner_refs[0].shape
    outer = outer_refs[0].shape[0]
    rows, width = inner + outer, outer // 2
    mix_high, mix_low = split(mix_ref[...])
    dot = functools.partial(jnp.dot, preferred_element_type=jnp.float32)

    def part(r):
        if width <= r < rows - width:
            return jnp.concatenate([ref[r - width] for ref in inner_refs], axis=0)
        return jnp.concatenate([ref[r if r < width else r - inner] for ref in outer_refs], axis=0)

    for r in range(0, rows, 2):
        high, low = split(jnp.concatenate([part(r), part(r + 1)], axis=1))
        fresh = dot(mix_high, high) + (dot(mix_high, low) + dot(mix_low, high))
        for i in range(2):
            out_ref[pl.ds(r + i, mem, stride=rows), :] = fresh[:, i * cols:(i + 1) * cols]


def shift(x, axis, step):
    count = lax.axis_size(axis)
    return lax.ppermute(x, axis, [(i, (i + step) % count) for i in range(count)])


def on_device(
    state, row_courant, col_courant, diffusion, obs_values, obs_variance, obs_offsets, owners
):
    mem, rows, cols = state.shape
    ens = lax.axis_size("ens")
    members = mem * ens
    observed = obs_values.shape[1]
    width = FSTEPS
    f32 = functools.partial(jax.ShapeDtypeStruct, dtype=jnp.float32)
    scratch = functools.partial(pltpu.VMEM, dtype=jnp.float32)
    place = lax.axis_index("dom").astype(jnp.int32).reshape(1)
    mixers = jnp.stack([
        1.0 - row_courant - col_courant - 4.0 * diffusion,
        row_courant + diffusion,
        col_courant + diffusion,
        diffusion,
    ])
    edge = f32((width, mem + 8, cols))
    top, upper, lower, bottom, inner = pl.pallas_call(
        inner_kernel,
        out_shape=(edge,) * 4 + (f32((rows - 2 * width, mem, cols)),),
        in_specs=[VMEM] * 2,
        out_specs=(VMEM,) * 5,
        scratch_shapes=[scratch((rows, mem, cols))] * 2,
        compiler_params=PARAMS,
        cost_estimate=estimate(3),
        name="inner",
    )(state.reshape(mem * rows, cols), mixers)
    up = shift(bottom, "dom", 1)
    down = shift(top, "dom", -1)
    outer, seen = pl.pallas_call(
        outer_kernel,
        out_shape=(f32((2 * width, mem, cols)), f32((mem, observed))),
        in_specs=[SMEM] * 2 + [VMEM] * 8,
        out_specs=(VMEM, VMEM),
        scratch_shapes=[scratch((3 * width, mem, cols))] * 2,
        compiler_params=PARAMS,
        cost_estimate=estimate(2),
        name="outer",
    )(place, owners, obs_offsets, up, top, upper, lower, bottom, down, inner)

    seens = [seen] + [shift(seen, "ens", k) for k in range(1, ens)]
    gram = pl.pallas_call(
        gram_kernel,
        out_shape=f32((members + 8, members)),
        in_specs=[SMEM] * 2 + [VMEM] * (2 + ens),
        out_specs=VMEM,
        compiler_params=PARAMS,
        cost_estimate=estimate(1),
        name="gram",
    )(place, owners, obs_values, obs_variance, *seens)
    grams = lax.all_gather(gram, "dom")

    def around(part):
        slots = [part] * ens
        for j in range(1, ens // 2 + 1):
            slots[j] = shift(slots[j - 1], "ens", 1)
        for j in range(1, (ens - 1) // 2 + 1):
            slots[ens - j] = shift(slots[(ens - j + 1) % ens], "ens", -1)
        return slots

    fields = [x for pair in zip(around(inner), around(outer)) for x in pair]

    mix = pl.pallas_call(
        chain_kernel,
        out_shape=f32((mem, members)),
        in_specs=[SMEM, VMEM],
        out_specs=VMEM,
        compiler_params=PARAMS,
        cost_estimate=estimate(CHAIN_US),
        name="chain",
    )(owners, grams)
    out = pl.pallas_call(
        apply_kernel,
        out_shape=f32((mem * rows, cols)),
        in_specs=[VMEM] * (1 + 2 * ens),
        out_specs=VMEM,
        compiler_params=PARAMS,
        cost_estimate=estimate(2),
        name="apply",
    )(mix, *fields)
    return out.reshape(mem, rows, cols)


def solution(mesh):
    return jax.shard_map(
        on_device,
        mesh=mesh,
        in_specs=(
            P("ens", "dom", None),
            P("dom", None),
            P("dom", None),
            P("dom", None),
            P(),
            P(),
            P(),
            P(),
        ),
        out_specs=P("ens", "dom", None),
        check_vma=False,
    )
```

```python
import functools

import jax
import jax.numpy as jnp
from jax import lax
from jax.experimental import pallas as pl
from jax.experimental.pallas import tpu as pltpu
from jax.sharding import PartitionSpec as P

FSTEPS = 4
TOLERANCE = 1e-6
WIDE_BOUND = 16.0
CHAIN_US = 2
EARLY_US = 0.1
HIGHEST = lax.Precision.HIGHEST
NN = (((1,), (0,)), ((), ()))
NT = (((1,), (1,)), ((), ()))

VMEM = pl.BlockSpec(memory_space=pltpu.VMEM)
SMEM = pl.BlockSpec(memory_space=pltpu.SMEM)
ANY = pl.BlockSpec(memory_space=pl.ANY)
PARAMS = pltpu.CompilerParams(vmem_limit_bytes=40 * 1024 * 1024)


def own_batch(place_ref, owners_ref):
    batch = jnp.int32(0)
    for i in range(owners_ref.shape[0]):
        batch = jnp.where(owners_ref[i] == place_ref[0], i, batch)
    return batch


def estimate(micros):
    return pl.CostEstimate(flops=int(1.15e9 * micros), bytes_accessed=0, transcendentals=0)


def rows_kernel(place_ref, owners_ref, offsets_ref, obs_ref, var_ref, cells_ref, own_ref):
    batch = pl.ds(own_batch(place_ref, owners_ref), 1)
    cells_ref[...] = jnp.broadcast_to(offsets_ref[batch, :], cells_ref.shape)
    own_ref[:8] = jnp.broadcast_to(obs_ref[batch, :], cells_ref.shape)
    own_ref[8:] = jnp.broadcast_to(var_ref[batch, :], cells_ref.shape)


def advance(load, coef, store, count, scratches):
    for step in range(1, FSTEPS + 1):
        source = load if step == 1 else scratches[step % 2].__getitem__
        for r in range(step, count - step):
            x = source(r)
            cols = x.shape[1]
            here, upper, side, lower = coef(r)
            fresh = (
                here * x
                + upper * source(r - 1)
                + side * pltpu.roll(x, 1, 1)
                + lower * (source(r + 1) + pltpu.roll(x, cols - 1, 1))
            )
            if step == FSTEPS:
                store(r, fresh)
            else:
                scratches[(step + 1) % 2][r] = fresh


def inner_kernel(
    state_ref, row_ref, col_ref, diff_ref, top_ref, upper_ref, lower_ref, bottom_ref, inner_ref,
    coef_ref, a_ref, b_ref,
):
    width = FSTEPS
    rows, mem, cols = a_ref.shape
    count = coef_ref.shape[0]
    row_c, col_c, diff_c = row_ref[...], col_ref[...], diff_ref[...]
    coef_ref[0] = 1.0 - row_c - col_c - 4.0 * diff_c
    coef_ref[1] = row_c + diff_c
    coef_ref[2] = col_c + diff_c
    coef_ref[3] = diff_c

    def load(r):
        return state_ref[pl.ds(r, mem, stride=rows), :]

    def coef(r):
        return [coef_ref[i, r:r + 1, :] for i in range(count)]

    blocks = (top_ref, 0), (upper_ref, width), (lower_ref, rows - 2 * width), (bottom_ref, rows - width)
    for ref, base in blocks:
        for r in range(width):
            ref[r, :mem, :] = load(base + r)
            for i, row in enumerate(coef(base + r)):
                ref[r, mem + i:mem + i + 1, :] = row
            ref[r, mem + count:, :] = jnp.zeros((ref.shape[1] - mem - count, cols), jnp.float32)

    def store(r, value):
        inner_ref[r - width] = value

    advance(load, coef, store, rows, (a_ref, b_ref))


def split3(x):
    high, rest = x.astype(jnp.bfloat16), x
    rest = rest - high.astype(jnp.float32)
    middle = rest.astype(jnp.bfloat16)
    return high, middle, (rest - middle.astype(jnp.float32)).astype(jnp.bfloat16)


def outer_kernel(
    cells_ref, up_ref, top_ref, upper_ref, lower_ref, bottom_ref, down_ref,
    inner_ref, outer_ref, seen_ref, a_ref, b_ref,
):
    width = FSTEPS
    inner, mem, cols = inner_ref.shape
    rows = inner + 2 * width
    observed = seen_ref.shape[1]

    for side, refs in enumerate(((up_ref, top_ref, upper_ref), (lower_ref, bottom_ref, down_ref))):

        def load(r, refs=refs):
            return refs[r // width][r % width, :mem, :]

        def coef(r, refs=refs):
            return [refs[r // width][r % width, mem + i:mem + i + 1, :] for i in range(4)]

        def store(r, value, side=side):
            outer_ref[side * width + r - width] = value

        advance(load, coef, store, 3 * width, (a_ref, b_ref))

    def field(r):
        if width <= r < rows - width:
            return inner_ref[r - width]
        return outer_ref[r if r < width else r - inner]

    cells = cells_ref[:1, :]
    index = lax.broadcasted_iota(jnp.int32, (2 * cols, observed), 0)
    total = jnp.zeros((3 * mem, observed), jnp.float32)
    for r in range(0, rows, 2):
        parts = jnp.concatenate(split3(jnp.concatenate([field(r), field(r + 1)], axis=1)), axis=0)
        chosen = (index == cells - r * cols).astype(jnp.float32).astype(jnp.bfloat16)
        total = total + jnp.dot(parts, chosen, preferred_element_type=jnp.float32)
    seen_ref[...] = total[:mem] + total[mem:2 * mem] + total[2 * mem:]


def gram_kernel(own_ref, *refs):
    seen_refs, out_ref = refs[:-1], refs[-1]
    seen = jnp.concatenate([ref[...] for ref in seen_refs], axis=0)
    members, count = seen.shape
    ybar = jnp.mean(seen, axis=0, keepdims=True)
    anom = seen - ybar
    weight = 1.0 / (own_ref[8:9, :] * (members - 1.0))
    gap = own_ref[:1, :] - ybar
    left = jnp.concatenate([anom * weight, jnp.broadcast_to(gap * weight, (8, count))], axis=0)
    out_ref[...] = lax.dot_general(
        left, anom, NT, precision=HIGHEST, preferred_element_type=jnp.float32
    )


def split(x):
    high = x.astype(jnp.bfloat16)
    return high, (x - high.astype(jnp.float32)).astype(jnp.bfloat16)


def product(wide, a, b, dims=NN):
    dot = functools.partial(
        lax.dot_general, dimension_numbers=dims, preferred_element_type=jnp.float32
    )
    if wide:
        return dot(a, b, precision=HIGHEST)
    a_high, a_low = split(a)
    b_high, b_low = split(b)
    return dot(a_high, b_high) + (dot(a_high, b_low) + dot(a_low, b_high))


def chain_kernel(soon, late, owners_ref, gram_ref, soon_ref, late_ref):
    mem = soon_ref.shape[0]
    members = gram_ref.shape[2]
    batches = owners_ref.shape[0]
    eye = (
        lax.broadcasted_iota(jnp.int32, (members, members), 0)
        == lax.broadcasted_iota(jnp.int32, (members, members), 1)
    ).astype(jnp.float32)

    def chain(wide):
        mul = functools.partial(product, wide)
        trans = mean_row = forward = None
        for b in range(batches):
            gram = gram_ref[owners_ref[b], :members, :]
            lead = gram_ref[owners_ref[b], members:members + 8, :]
            if b == 0:
                excess, vec = gram, lead
                trans, mean_row = eye, jnp.zeros_like(lead)
            else:
                first = mul(jnp.concatenate([gram, lead], axis=0), trans)
                second = mul(jnp.concatenate([forward, mean_row], axis=0), first[:members])
                excess = second[:members]
                vec = first[members:] - second[members:]
            bound = 1.0 + jnp.max(jnp.sum(jnp.abs(excess), axis=0, keepdims=True))
            scale = 2.0 / (1.0 + bound)
            off = (bound - 1.0) / (bound + 1.0)
            rest = (1.0 - scale) * eye - scale * excess
            power = scale * jnp.concatenate([trans, vec], axis=0)

            def unfinished(carry):
                off = carry[0]
                return off * off / (2.0 - off * off) > TOLERANCE

            def refine(carry):
                off, rest, power = carry
                factor = 2.0 / (2.0 - off * off)
                both = mul(jnp.concatenate([rest, power], axis=0), rest)
                rest = factor * both[:members] + (1.0 - factor) * eye
                power = factor * (power + both[members:])
                return off * off / (2.0 - off * off), rest, power

            off, rest, power = lax.while_loop(unfinished, refine, (off, rest, power))
            power = 2.0 / (2.0 - off * off) * (power + mul(power, rest))
            move = power[members:]
            mean_row = mean_row + (move if b == 0 else mul(move, forward))
            trans = 0.5 * (trans + power[:members])
            forward = trans.T
        mix = forward[:mem] + mean_row[:1]
        for ref, slots in ((soon_ref, soon), (late_ref, late)):
            parts = [mix[:, j * mem:(j + 1) * mem] for j in slots]
            ref[...] = jnp.concatenate(parts, axis=1)

    worst = jnp.float32(0.0)
    for b in range(batches):
        gram = gram_ref[owners_ref[b], :members, :]
        worst = jnp.maximum(worst, jnp.max(jnp.sum(jnp.abs(gram), axis=0, keepdims=True)))
    pl.when(worst > WIDE_BOUND)(lambda: chain(True))
    pl.when(jnp.logical_not(worst > WIDE_BOUND))(lambda: chain(False))


def row_of(pair, r):
    inner_ref, outer_ref = pair
    inner, width = inner_ref.shape[0], outer_ref.shape[0] // 2
    if width <= r < inner + width:
        return inner_ref[r - width]
    return outer_ref[r if r < width else r - inner]


def share(mix, pairs, r):
    high, low = split(mix)
    x = jnp.concatenate(
        [jnp.concatenate([row_of(pair, r + i) for pair in pairs], axis=0) for i in range(2)], axis=1
    )
    x_high, x_low = split(x)
    dot = functools.partial(jnp.dot, preferred_element_type=jnp.float32)
    return dot(high, x_high) + (dot(high, x_low) + dot(low, x_high))


def early_kernel(mix_ref, *refs):
    field_refs, sum_ref = refs[:-1], refs[-1]
    pairs = list(zip(field_refs[::2], field_refs[1::2]))
    for r in range(0, 2 * sum_ref.shape[0], 2):
        sum_ref[r // 2] = share(mix_ref[...], pairs, r)


def late_kernel(mix_ref, sum_ref, *refs):
    field_refs, out_ref, stage_ref, sems = refs[:-3], refs[-3], refs[-2], refs[-1]
    pairs = list(zip(field_refs[::2], field_refs[1::2]))
    rows, cols = stage_ref.shape[1:]
    chunk = rows // sems.shape[0]
    copies = []
    for r in range(0, rows, 2):
        fresh = sum_ref[r // 2] + share(mix_ref[...], pairs, r)
        for i in range(2):
            stage_ref[:, r + i, :] = fresh[:, i * cols:(i + 1) * cols]
        if (r + 2) % chunk == 0:
            block = pl.ds(r + 2 - chunk, chunk)
            copy = pltpu.make_async_copy(
                stage_ref.at[:, block, :], out_ref.at[:, block, :], sems.at[len(copies)]
            )
            copy.start()
            copies.append(copy)
    for copy in copies:
        copy.wait()


def shift(x, axis, step):
    count = lax.axis_size(axis)
    return lax.ppermute(x, axis, [(i, (i + step) % count) for i in range(count)])


def on_device(
    state, row_courant, col_courant, diffusion, obs_values, obs_variance, obs_offsets, owners
):
    mem, rows, cols = state.shape
    ens = lax.axis_size("ens")
    members = mem * ens
    observed = obs_values.shape[1]
    width = FSTEPS
    f32 = functools.partial(jax.ShapeDtypeStruct, dtype=jnp.float32)
    scratch = functools.partial(pltpu.VMEM, dtype=jnp.float32)
    place = lax.axis_index("dom").astype(jnp.int32).reshape(1)
    staged = jnp.pad(state, ((0, 1), (0, 0), (0, 0))).reshape(-1, cols)
    edge = f32((width, mem + 8, cols))
    cells, own = pl.pallas_call(
        rows_kernel,
        out_shape=(jax.ShapeDtypeStruct((8, observed), jnp.int32), f32((16, observed))),
        in_specs=[SMEM] * 2 + [VMEM] * 3,
        out_specs=(VMEM, VMEM),
        compiler_params=PARAMS,
        cost_estimate=estimate(1),
        name="rows",
    )(place, owners, obs_offsets, obs_values, obs_variance)
    top, upper, lower, bottom, inner = pl.pallas_call(
        inner_kernel,
        out_shape=(edge,) * 4 + (f32((rows - 2 * width, mem, cols)),),
        in_specs=[VMEM] * 4,
        out_specs=(VMEM,) * 5,
        scratch_shapes=[scratch((4, rows, cols))] + [scratch((rows, mem, cols))] * 2,
        compiler_params=PARAMS,
        cost_estimate=estimate(3),
        name="inner",
    )(staged, row_courant, col_courant, diffusion)
    up = shift(bottom, "dom", 1)
    down = shift(top, "dom", -1)
    outer, seen = pl.pallas_call(
        outer_kernel,
        out_shape=(f32((2 * width, mem, cols)), f32((mem, observed))),
        in_specs=[VMEM] * 8,
        out_specs=(VMEM, VMEM),
        scratch_shapes=[scratch((3 * width, mem, cols))] * 2,
        compiler_params=PARAMS,
        cost_estimate=estimate(2),
        name="outer",
    )(cells, up, top, upper, lower, bottom, down, inner)

    seens = [seen] + [shift(seen, "ens", k) for k in range(1, ens)]
    gram = pl.pallas_call(
        gram_kernel,
        out_shape=f32((members + 8, members)),
        in_specs=[VMEM] * (1 + ens),
        out_specs=VMEM,
        compiler_params=PARAMS,
        cost_estimate=estimate(1),
        name="gram",
    )(own, *seens)
    grams = lax.all_gather(gram, "dom")

    def around(part):
        slots = [part] * ens
        for j in range(1, ens // 2 + 1):
            slots[j] = shift(slots[j - 1], "ens", 1)
        for j in range(1, (ens - 1) // 2 + 1):
            slots[ens - j] = shift(slots[(ens - j + 1) % ens], "ens", -1)
        return slots

    slots = list(zip(around(inner), around(outer)))
    late = list(range(2, ens - 1))
    soon = [j for j in range(ens) if j not in late]

    mix_soon, mix_late = pl.pallas_call(
        functools.partial(chain_kernel, soon, late),
        out_shape=(f32((mem, mem * len(soon))), f32((mem, mem * len(late)))),
        in_specs=[SMEM, VMEM],
        out_specs=(VMEM, VMEM),
        compiler_params=PARAMS,
        cost_estimate=estimate(CHAIN_US),
        name="chain",
    )(owners, grams)
    sums = pl.pallas_call(
        early_kernel,
        out_shape=f32((rows // 2, mem, 2 * cols)),
        in_specs=[VMEM] * (1 + 2 * len(soon)),
        out_specs=VMEM,
        compiler_params=PARAMS,
        cost_estimate=estimate(EARLY_US),
        name="early",
    )(mix_soon, *[x for j in soon for x in slots[j]])
    return pl.pallas_call(
        late_kernel,
        out_shape=f32((mem, rows, cols)),
        in_specs=[VMEM] * (2 + 2 * len(late)),
        out_specs=ANY,
        scratch_shapes=[scratch((mem, rows, cols)), pltpu.SemaphoreType.DMA((rows // 8,))],
        compiler_params=PARAMS,
        cost_estimate=estimate(1),
        name="late",
    )(mix_late, sums, *[x for j in late for x in slots[j]])


def solution(mesh):
    return jax.shard_map(
        on_device,
        mesh=mesh,
        in_specs=(
            P("ens", "dom", None),
            P("dom", None),
            P("dom", None),
            P("dom", None),
            P(),
            P(),
            P(),
            P(),
        ),
        out_specs=P("ens", "dom", None),
        check_vma=False,
    )
```

```python
import functools

import jax
import jax.numpy as jnp
from jax import lax
from jax.experimental import pallas as pl
from jax.experimental.pallas import tpu as pltpu
from jax.sharding import PartitionSpec as P

FSTEPS = 4
TOLERANCE = 1e-6
WIDE_BOUND = 16.0
CHAIN_US = 2
EARLY_US = 0.1
HIGHEST = lax.Precision.HIGHEST
NN = (((1,), (0,)), ((), ()))
NT = (((1,), (1,)), ((), ()))

VMEM = pl.BlockSpec(memory_space=pltpu.VMEM)
SMEM = pl.BlockSpec(memory_space=pltpu.SMEM)
ANY = pl.BlockSpec(memory_space=pl.ANY)
PARAMS = pltpu.CompilerParams(vmem_limit_bytes=40 * 1024 * 1024)


def own_batch(place_ref, owners_ref):
    batch = jnp.int32(0)
    for i in range(owners_ref.shape[0]):
        batch = jnp.where(owners_ref[i] == place_ref[0], i, batch)
    return batch


def estimate(micros):
    return pl.CostEstimate(flops=int(1.15e9 * micros), bytes_accessed=0, transcendentals=0)


def rows_kernel(place_ref, owners_ref, offsets_ref, obs_ref, var_ref, cells_ref, own_ref):
    batch = pl.ds(own_batch(place_ref, owners_ref), 1)
    cells_ref[...] = jnp.broadcast_to(offsets_ref[batch, :], cells_ref.shape)
    own_ref[:8] = jnp.broadcast_to(obs_ref[batch, :], cells_ref.shape)
    own_ref[8:] = jnp.broadcast_to(var_ref[batch, :], cells_ref.shape)


def advance(load, coef, store, count, scratches):
    for step in range(1, FSTEPS + 1):
        source = load if step == 1 else scratches[step % 2].__getitem__
        for r in range(step, count - step):
            x = source(r)
            cols = x.shape[1]
            here, upper, side, lower = coef(r)
            fresh = (
                here * x
                + upper * source(r - 1)
                + side * pltpu.roll(x, 1, 1)
                + lower * (source(r + 1) + pltpu.roll(x, cols - 1, 1))
            )
            if step == FSTEPS:
                store(r, fresh)
            else:
                scratches[(step + 1) % 2][r] = fresh


def inner_kernel(
    state_ref, row_ref, col_ref, diff_ref, top_ref, upper_ref, lower_ref, bottom_ref, inner_ref,
    coef_ref, a_ref, b_ref,
):
    width = FSTEPS
    rows, mem, cols = a_ref.shape
    count = coef_ref.shape[0]
    row_c, col_c, diff_c = row_ref[...], col_ref[...], diff_ref[...]
    coef_ref[0] = 1.0 - row_c - col_c - 4.0 * diff_c
    coef_ref[1] = row_c + diff_c
    coef_ref[2] = col_c + diff_c
    coef_ref[3] = diff_c

    def load(r):
        return state_ref[pl.ds(r, mem, stride=rows), :]

    def coef(r):
        return [coef_ref[i, r:r + 1, :] for i in range(count)]

    blocks = (top_ref, 0), (upper_ref, width), (lower_ref, rows - 2 * width), (bottom_ref, rows - width)
    for ref, base in blocks:
        for r in range(width):
            ref[r, :mem, :] = load(base + r)
            for i, row in enumerate(coef(base + r)):
                ref[r, mem + i:mem + i + 1, :] = row
            ref[r, mem + count:, :] = jnp.zeros((ref.shape[1] - mem - count, cols), jnp.float32)

    def store(r, value):
        inner_ref[r - width] = value

    advance(load, coef, store, rows, (a_ref, b_ref))


def split3(x):
    high, rest = x.astype(jnp.bfloat16), x
    rest = rest - high.astype(jnp.float32)
    middle = rest.astype(jnp.bfloat16)
    return high, middle, (rest - middle.astype(jnp.float32)).astype(jnp.bfloat16)


def outer_kernel(
    cells_ref, up_ref, top_ref, upper_ref, lower_ref, bottom_ref, down_ref,
    inner_ref, outer_ref, seen_ref, a_ref, b_ref,
):
    width = FSTEPS
    inner, mem, cols = inner_ref.shape
    rows = inner + 2 * width
    observed = seen_ref.shape[1]

    for side, refs in enumerate(((up_ref, top_ref, upper_ref), (lower_ref, bottom_ref, down_ref))):

        def load(r, refs=refs):
            return refs[r // width][r % width, :mem, :]

        def coef(r, refs=refs):
            return [refs[r // width][r % width, mem + i:mem + i + 1, :] for i in range(4)]

        def store(r, value, side=side):
            outer_ref[side * width + r - width] = value

        advance(load, coef, store, 3 * width, (a_ref, b_ref))

    def field(r):
        if width <= r < rows - width:
            return inner_ref[r - width]
        return outer_ref[r if r < width else r - inner]

    cells = cells_ref[:1, :]
    index = lax.broadcasted_iota(jnp.int32, (2 * cols, observed), 0)
    total = jnp.zeros((3 * mem, observed), jnp.float32)
    for r in range(0, rows, 2):
        parts = jnp.concatenate(split3(jnp.concatenate([field(r), field(r + 1)], axis=1)), axis=0)
        chosen = (index == cells - r * cols).astype(jnp.float32).astype(jnp.bfloat16)
        total = total + jnp.dot(parts, chosen, preferred_element_type=jnp.float32)
    seen_ref[...] = total[:mem] + total[mem:2 * mem] + total[2 * mem:]


def gram_kernel(own_ref, *refs):
    seen_refs, out_ref = refs[:-1], refs[-1]
    seen = jnp.concatenate([ref[...] for ref in seen_refs], axis=0)
    members, count = seen.shape
    ybar = jnp.mean(seen, axis=0, keepdims=True)
    anom = seen - ybar
    weight = 1.0 / (own_ref[8:9, :] * (members - 1.0))
    gap = own_ref[:1, :] - ybar
    left = jnp.concatenate([anom * weight, jnp.broadcast_to(gap * weight, (8, count))], axis=0)
    out_ref[...] = lax.dot_general(
        left, anom, NT, precision=HIGHEST, preferred_element_type=jnp.float32
    )


def split(x):
    high = x.astype(jnp.bfloat16)
    return high, (x - high.astype(jnp.float32)).astype(jnp.bfloat16)


def product(wide, a, b, dims=NN):
    dot = functools.partial(
        lax.dot_general, dimension_numbers=dims, preferred_element_type=jnp.float32
    )
    if wide:
        return dot(a, b, precision=HIGHEST)
    a_high, a_low = split(a)
    b_high, b_low = split(b)
    return dot(a_high, b_high) + (dot(a_high, b_low) + dot(a_low, b_high))


def chain_kernel(soon, late, owners_ref, gram_ref, soon_ref, late_ref):
    mem = soon_ref.shape[0]
    members = gram_ref.shape[2]
    batches = owners_ref.shape[0]
    eye = (
        lax.broadcasted_iota(jnp.int32, (members, members), 0)
        == lax.broadcasted_iota(jnp.int32, (members, members), 1)
    ).astype(jnp.float32)

    def chain(wide):
        mul = functools.partial(product, wide)
        trans = mean_row = forward = None
        for b in range(batches):
            gram = gram_ref[owners_ref[b], :members, :]
            lead = gram_ref[owners_ref[b], members:members + 8, :]
            if b == 0:
                excess, vec = gram, lead
                trans, mean_row = eye, jnp.zeros_like(lead)
            else:
                first = mul(jnp.concatenate([gram, lead], axis=0), trans)
                second = mul(jnp.concatenate([forward, mean_row], axis=0), first[:members])
                excess = second[:members]
                vec = first[members:] - second[members:]
            bound = 1.0 + jnp.max(jnp.sum(jnp.abs(excess), axis=0, keepdims=True))
            scale = 2.0 / (1.0 + bound)
            off = (bound - 1.0) / (bound + 1.0)
            rest = (1.0 - scale) * eye - scale * excess
            power = scale * jnp.concatenate([trans, vec], axis=0)

            def unfinished(carry):
                off = carry[0]
                return off * off / (2.0 - off * off) > TOLERANCE

            def refine(carry):
                off, rest, power = carry
                factor = 2.0 / (2.0 - off * off)
                both = mul(jnp.concatenate([rest, power], axis=0), rest)
                rest = factor * both[:members] + (1.0 - factor) * eye
                power = factor * (power + both[members:])
                return off * off / (2.0 - off * off), rest, power

            off, rest, power = lax.while_loop(unfinished, refine, (off, rest, power))
            power = 2.0 / (2.0 - off * off) * (power + mul(power, rest))
            move = power[members:]
            mean_row = mean_row + (move if b == 0 else mul(move, forward))
            trans = 0.5 * (trans + power[:members])
            forward = trans.T
        mix = forward[:mem] + mean_row[:1]
        mix = mix - (jnp.sum(mix, axis=1, keepdims=True) - 1.0) / members
        for ref, slots in ((soon_ref, soon), (late_ref, late)):
            parts = [mix[:, j * mem:(j + 1) * mem] for j in slots]
            ref[...] = jnp.concatenate(parts, axis=1)

    worst = jnp.float32(0.0)
    for b in range(batches):
        gram = gram_ref[owners_ref[b], :members, :]
        worst = jnp.maximum(worst, jnp.max(jnp.sum(jnp.abs(gram), axis=0, keepdims=True)))
    pl.when(worst > WIDE_BOUND)(lambda: chain(True))
    pl.when(jnp.logical_not(worst > WIDE_BOUND))(lambda: chain(False))


def row_of(pair, r):
    inner_ref, outer_ref = pair
    inner, width = inner_ref.shape[0], outer_ref.shape[0] // 2
    if width <= r < inner + width:
        return inner_ref[r - width]
    return outer_ref[r if r < width else r - inner]


def share(mix, pairs, r):
    high, low = split(mix)
    x = jnp.concatenate(
        [jnp.concatenate([row_of(pair, r + i) for pair in pairs], axis=0) for i in range(2)], axis=1
    )
    x_high, x_low = split(x)
    dot = functools.partial(jnp.dot, preferred_element_type=jnp.float32)
    return dot(high, x_high) + (dot(high, x_low) + dot(low, x_high))


def early_kernel(mix_ref, *refs):
    field_refs, sum_ref = refs[:-1], refs[-1]
    pairs = list(zip(field_refs[::2], field_refs[1::2]))
    for r in range(0, 2 * sum_ref.shape[0], 2):
        sum_ref[r // 2] = share(mix_ref[...], pairs, r)


def late_kernel(mix_ref, sum_ref, *refs):
    field_refs, out_ref, stage_ref, sems = refs[:-3], refs[-3], refs[-2], refs[-1]
    pairs = list(zip(field_refs[::2], field_refs[1::2]))
    rows, cols = stage_ref.shape[1:]
    chunk = rows // sems.shape[0]
    copies = []
    for r in range(0, rows, 2):
        fresh = sum_ref[r // 2] + share(mix_ref[...], pairs, r)
        for i in range(2):
            stage_ref[:, r + i, :] = fresh[:, i * cols:(i + 1) * cols]
        if (r + 2) % chunk == 0:
            block = pl.ds(r + 2 - chunk, chunk)
            copy = pltpu.make_async_copy(
                stage_ref.at[:, block, :], out_ref.at[:, block, :], sems.at[len(copies)]
            )
            copy.start()
            copies.append(copy)
    for copy in copies:
        copy.wait()


def shift(x, axis, step):
    count = lax.axis_size(axis)
    return lax.ppermute(x, axis, [(i, (i + step) % count) for i in range(count)])


def on_device(
    state, row_courant, col_courant, diffusion, obs_values, obs_variance, obs_offsets, owners
):
    mem, rows, cols = state.shape
    ens = lax.axis_size("ens")
    members = mem * ens
    observed = obs_values.shape[1]
    width = FSTEPS
    f32 = functools.partial(jax.ShapeDtypeStruct, dtype=jnp.float32)
    scratch = functools.partial(pltpu.VMEM, dtype=jnp.float32)
    place = lax.axis_index("dom").astype(jnp.int32).reshape(1)
    staged = jnp.pad(state, ((0, 1), (0, 0), (0, 0))).reshape(-1, cols)
    edge = f32((width, mem + 8, cols))
    cells, own = pl.pallas_call(
        rows_kernel,
        out_shape=(jax.ShapeDtypeStruct((8, observed), jnp.int32), f32((16, observed))),
        in_specs=[SMEM] * 2 + [VMEM] * 3,
        out_specs=(VMEM, VMEM),
        compiler_params=PARAMS,
        cost_estimate=estimate(1),
        name="rows",
    )(place, owners, obs_offsets, obs_values, obs_variance)
    top, upper, lower, bottom, inner = pl.pallas_call(
        inner_kernel,
        out_shape=(edge,) * 4 + (f32((rows - 2 * width, mem, cols)),),
        in_specs=[VMEM] * 4,
        out_specs=(VMEM,) * 5,
        scratch_shapes=[scratch((4, rows, cols))] + [scratch((rows, mem, cols))] * 2,
        compiler_params=PARAMS,
        cost_estimate=estimate(3),
        name="inner",
    )(staged, row_courant, col_courant, diffusion)
    up = shift(bottom, "dom", 1)
    down = shift(top, "dom", -1)
    outer, seen = pl.pallas_call(
        outer_kernel,
        out_shape=(f32((2 * width, mem, cols)), f32((mem, observed))),
        in_specs=[VMEM] * 8,
        out_specs=(VMEM, VMEM),
        scratch_shapes=[scratch((3 * width, mem, cols))] * 2,
        compiler_params=PARAMS,
        cost_estimate=estimate(2),
        name="outer",
    )(cells, up, top, upper, lower, bottom, down, inner)

    seens = [seen] + [shift(seen, "ens", k) for k in range(1, ens)]
    gram = pl.pallas_call(
        gram_kernel,
        out_shape=f32((members + 8, members)),
        in_specs=[VMEM] * (1 + ens),
        out_specs=VMEM,
        compiler_params=PARAMS,
        cost_estimate=estimate(1),
        name="gram",
    )(own, *seens)
    grams = lax.all_gather(gram, "dom")

    def around(part):
        slots = [part] * ens
        for j in range(1, ens // 2 + 1):
            slots[j] = shift(slots[j - 1], "ens", 1)
        for j in range(1, (ens - 1) // 2 + 1):
            slots[ens - j] = shift(slots[(ens - j + 1) % ens], "ens", -1)
        return slots

    slots = list(zip(around(inner), around(outer)))
    late = list(range(2, ens - 1))
    soon = [j for j in range(ens) if j not in late]

    mix_soon, mix_late = pl.pallas_call(
        functools.partial(chain_kernel, soon, late),
        out_shape=(f32((mem, mem * len(soon))), f32((mem, mem * len(late)))),
        in_specs=[SMEM, VMEM],
        out_specs=(VMEM, VMEM),
        compiler_params=PARAMS,
        cost_estimate=estimate(CHAIN_US),
        name="chain",
    )(owners, grams)
    sums = pl.pallas_call(
        early_kernel,
        out_shape=f32((rows // 2, mem, 2 * cols)),
        in_specs=[VMEM] * (1 + 2 * len(soon)),
        out_specs=VMEM,
        compiler_params=PARAMS,
        cost_estimate=estimate(EARLY_US),
        name="early",
    )(mix_soon, *[x for j in soon for x in slots[j]])
    return pl.pallas_call(
        late_kernel,
        out_shape=f32((mem, rows, cols)),
        in_specs=[VMEM] * (2 + 2 * len(late)),
        out_specs=ANY,
        scratch_shapes=[scratch((mem, rows, cols)), pltpu.SemaphoreType.DMA((rows // 8,))],
        compiler_params=PARAMS,
        cost_estimate=estimate(1),
        name="late",
    )(mix_late, sums, *[x for j in late for x in slots[j]])


def solution(mesh):
    return jax.shard_map(
        on_device,
        mesh=mesh,
        in_specs=(
            P("ens", "dom", None),
            P("dom", None),
            P("dom", None),
            P("dom", None),
            P(),
            P(),
            P(),
            P(),
        ),
        out_specs=P("ens", "dom", None),
        check_vma=False,
    )
```

```python
import functools

import jax
import jax.numpy as jnp
from jax import lax
from jax.experimental import pallas as pl
from jax.experimental.pallas import tpu as pltpu
from jax.sharding import PartitionSpec as P

FSTEPS = 4
TOLERANCE = 1e-6
WIDE_BOUND = 16.0
CHAIN_US = 2
EARLY_US = 0.1
HIGHEST = lax.Precision.HIGHEST
NN = (((1,), (0,)), ((), ()))
NT = (((1,), (1,)), ((), ()))

VMEM = pl.BlockSpec(memory_space=pltpu.VMEM)
SMEM = pl.BlockSpec(memory_space=pltpu.SMEM)
ANY = pl.BlockSpec(memory_space=pl.ANY)
PARAMS = pltpu.CompilerParams(vmem_limit_bytes=40 * 1024 * 1024)


def own_batch(place_ref, owners_ref):
    batch = jnp.int32(0)
    for i in range(owners_ref.shape[0]):
        batch = jnp.where(owners_ref[i] == place_ref[0], i, batch)
    return batch


def estimate(micros):
    return pl.CostEstimate(flops=int(1.15e9 * micros), bytes_accessed=0, transcendentals=0)


def rows_kernel(place_ref, owners_ref, offsets_ref, obs_ref, var_ref, cells_ref, own_ref):
    batch = pl.ds(own_batch(place_ref, owners_ref), 1)
    cells_ref[...] = jnp.broadcast_to(offsets_ref[batch, :], cells_ref.shape)
    own_ref[:8] = jnp.broadcast_to(obs_ref[batch, :], cells_ref.shape)
    own_ref[8:] = jnp.broadcast_to(var_ref[batch, :], cells_ref.shape)


def advance(load, coef, store, count, scratches):
    for step in range(1, FSTEPS + 1):
        source = functools.cache(load) if step == 1 else scratches[step % 2].__getitem__
        for r in range(step, count - step):
            x = source(r)
            cols = x.shape[1]
            here, upper, side, lower = coef(r)
            fresh = (
                here * x
                + upper * source(r - 1)
                + side * pltpu.roll(x, 1, 1)
                + lower * (source(r + 1) + pltpu.roll(x, cols - 1, 1))
            )
            if step == FSTEPS:
                store(r, fresh)
            else:
                scratches[(step + 1) % 2][r] = fresh


def inner_kernel(
    state_ref, row_ref, col_ref, diff_ref, inner_ref, coef_ref, a_ref, b_ref
):
    rows, mem, _ = a_ref.shape
    row_c, col_c, diff_c = row_ref[...], col_ref[...], diff_ref[...]
    coef_ref[0] = 1.0 - row_c - col_c - 4.0 * diff_c
    coef_ref[1] = row_c + diff_c
    coef_ref[2] = col_c + diff_c
    coef_ref[3] = diff_c

    def load(r):
        return state_ref[pl.ds(r, mem, stride=rows), :]

    def coef(r):
        return [coef_ref[i, r:r + 1, :] for i in range(4)]

    def store(r, value):
        inner_ref[r - FSTEPS] = value

    advance(load, coef, store, rows, (a_ref, b_ref))


def border_kernel(state_ref, coef_ref, top_ref, upper_ref, lower_ref, bottom_ref):
    width, lanes, cols = top_ref.shape
    count, rows, _ = coef_ref.shape
    mem = lanes - 8
    bases = 0, width, rows - 2 * width, rows - width
    for ref, base in zip((top_ref, upper_ref, lower_ref, bottom_ref), bases):
        for r in range(width):
            row = base + r
            ref[r, :mem, :] = state_ref[pl.ds(row, mem, stride=rows), :]
            for i in range(count):
                ref[r, mem + i:mem + i + 1, :] = coef_ref[i, row:row + 1, :]
            ref[r, mem + count:, :] = jnp.zeros((8 - count, cols), jnp.float32)


def split3(x):
    high, rest = x.astype(jnp.bfloat16), x
    rest = rest - high.astype(jnp.float32)
    middle = rest.astype(jnp.bfloat16)
    return high, middle, (rest - middle.astype(jnp.float32)).astype(jnp.bfloat16)


def outer_kernel(
    cells_ref, up_ref, top_ref, upper_ref, lower_ref, bottom_ref, down_ref,
    inner_ref, outer_ref, seen_ref, a_ref, b_ref,
):
    width = FSTEPS
    inner, mem, cols = inner_ref.shape
    rows = inner + 2 * width
    observed = seen_ref.shape[1]

    for side, refs in enumerate(((up_ref, top_ref, upper_ref), (lower_ref, bottom_ref, down_ref))):

        def load(r, refs=refs):
            return refs[r // width][r % width, :mem, :]

        def coef(r, refs=refs):
            return [refs[r // width][r % width, mem + i:mem + i + 1, :] for i in range(4)]

        def store(r, value, side=side):
            outer_ref[side * width + r - width] = value

        advance(load, coef, store, 3 * width, (a_ref, b_ref))

    def field(r):
        if width <= r < rows - width:
            return inner_ref[r - width]
        return outer_ref[r if r < width else r - inner]

    cells = cells_ref[:1, :]
    index = lax.broadcasted_iota(jnp.int32, (2 * cols, observed), 0)
    total = jnp.zeros((3 * mem, observed), jnp.float32)
    for r in range(0, rows, 2):
        parts = jnp.concatenate(split3(jnp.concatenate([field(r), field(r + 1)], axis=1)), axis=0)
        chosen = (index == cells - r * cols).astype(jnp.float32).astype(jnp.bfloat16)
        total = total + jnp.dot(parts, chosen, preferred_element_type=jnp.float32)
    seen_ref[...] = total[:mem] + total[mem:2 * mem] + total[2 * mem:]


def gram_kernel(own_ref, *refs):
    seen_refs, out_ref = refs[:-1], refs[-1]
    seen = jnp.concatenate([ref[...] for ref in seen_refs], axis=0)
    members, count = seen.shape
    ybar = jnp.mean(seen, axis=0, keepdims=True)
    anom = seen - ybar
    weight = 1.0 / (own_ref[8:9, :] * (members - 1.0))
    gap = own_ref[:1, :] - ybar
    left = jnp.concatenate([anom * weight, jnp.broadcast_to(gap * weight, (8, count))], axis=0)
    out_ref[...] = lax.dot_general(
        left, anom, NT, precision=HIGHEST, preferred_element_type=jnp.float32
    )


def split(x):
    high = x.astype(jnp.bfloat16)
    return high, (x - high.astype(jnp.float32)).astype(jnp.bfloat16)


def product(wide, a, b, dims=NN):
    dot = functools.partial(
        lax.dot_general, dimension_numbers=dims, preferred_element_type=jnp.float32
    )
    if wide:
        return dot(a, b, precision=HIGHEST)
    a_high, a_low = split(a)
    b_high, b_low = split(b)
    return dot(a_high, b_high) + (dot(a_high, b_low) + dot(a_low, b_high))


def chain_kernel(soon, late, owners_ref, gram_ref, soon_ref, late_ref):
    mem = soon_ref.shape[0]
    members = gram_ref.shape[2]
    batches = owners_ref.shape[0]
    eye = (
        lax.broadcasted_iota(jnp.int32, (members, members), 0)
        == lax.broadcasted_iota(jnp.int32, (members, members), 1)
    ).astype(jnp.float32)

    def chain(wide):
        mul = functools.partial(product, wide)
        trans = mean_row = forward = None
        for b in range(batches):
            gram = gram_ref[owners_ref[b], :members, :]
            lead = gram_ref[owners_ref[b], members:members + 8, :]
            if b == 0:
                excess, vec = gram, lead
                trans, mean_row = eye, jnp.zeros_like(lead)
            else:
                first = mul(jnp.concatenate([gram, lead], axis=0), trans)
                second = mul(jnp.concatenate([forward, mean_row], axis=0), first[:members])
                excess = second[:members]
                vec = first[members:] - second[members:]
            bound = 1.0 + jnp.max(jnp.sum(jnp.abs(excess), axis=0, keepdims=True))
            scale = 2.0 / (1.0 + bound)
            off = (bound - 1.0) / (bound + 1.0)
            rest = (1.0 - scale) * eye - scale * excess
            power = scale * jnp.concatenate([trans, vec], axis=0)

            def unfinished(carry):
                off = carry[0]
                return off * off / (2.0 - off * off) > TOLERANCE

            def refine(carry):
                off, rest, power = carry
                factor = 2.0 / (2.0 - off * off)
                both = mul(jnp.concatenate([rest, power], axis=0), rest)
                rest = factor * both[:members] + (1.0 - factor) * eye
                power = factor * (power + both[members:])
                return off * off / (2.0 - off * off), rest, power

            off, rest, power = lax.while_loop(unfinished, refine, (off, rest, power))
            power = 2.0 / (2.0 - off * off) * (power + mul(power, rest))
            move = power[members:]
            mean_row = mean_row + (move if b == 0 else mul(move, forward))
            trans = 0.5 * (trans + power[:members])
            forward = trans.T
        mix = forward[:mem] + mean_row[:1]
        mix = mix - (jnp.sum(mix, axis=1, keepdims=True) - 1.0) / members
        for ref, slots in ((soon_ref, soon), (late_ref, late)):
            parts = [mix[:, j * mem:(j + 1) * mem] for j in slots]
            ref[...] = jnp.concatenate(parts, axis=1)

    worst = jnp.float32(0.0)
    for b in range(batches):
        gram = gram_ref[owners_ref[b], :members, :]
        worst = jnp.maximum(worst, jnp.max(jnp.sum(jnp.abs(gram), axis=0, keepdims=True)))
    pl.when(worst > WIDE_BOUND)(lambda: chain(True))
    pl.when(jnp.logical_not(worst > WIDE_BOUND))(lambda: chain(False))


def row_of(pair, r):
    if len(pair) == 1:
        return pair[0][r - FSTEPS]
    inner_ref, outer_ref = pair
    inner, width = inner_ref.shape[0], outer_ref.shape[0] // 2
    if width <= r < inner + width:
        return inner_ref[r - width]
    return outer_ref[r if r < width else r - inner]


def share(mix, pairs, r):
    high, low = split(mix)
    x = jnp.concatenate(
        [jnp.concatenate([row_of(pair, r + i) for pair in pairs], axis=0) for i in range(2)], axis=1
    )
    x_high, x_low = split(x)
    dot = functools.partial(jnp.dot, preferred_element_type=jnp.float32)
    return dot(high, x_high) + (dot(high, x_low) + dot(low, x_high))


def early_kernel(mix_ref, *refs):
    field_refs, sum_ref = refs[:-1], refs[-1]
    pairs = list(zip(field_refs[::2], field_refs[1::2]))
    for r in range(0, 2 * sum_ref.shape[0], 2):
        sum_ref[r // 2] = share(mix_ref[...], pairs, r)


def late_kernel(blocks, pieces, mix_ref, sum_ref, *refs):
    out_ref, stage_ref, sems = refs[-3:]
    groups = [refs[i:i + pieces] for i in range(0, mix_ref.shape[1] // stage_ref.shape[0] * pieces, pieces)]
    chunk, cols = 8, stage_ref.shape[2]
    copies = []
    for block in blocks:
        for r in range(block, block + chunk, 2):
            fresh = sum_ref[r // 2] + share(mix_ref[...], groups, r)
            for i in range(2):
                stage_ref[:, r + i, :] = fresh[:, i * cols:(i + 1) * cols]
        rows = pl.ds(block, chunk)
        copy = pltpu.make_async_copy(
            stage_ref.at[:, rows, :], out_ref.at[:, rows, :], sems.at[len(copies)]
        )
        copy.start()
        copies.append(copy)
    for copy in copies:
        copy.wait()


def shift(x, axis, step):
    count = lax.axis_size(axis)
    return lax.ppermute(x, axis, [(i, (i + step) % count) for i in range(count)])


def on_device(
    state, row_courant, col_courant, diffusion, obs_values, obs_variance, obs_offsets, owners
):
    mem, rows, cols = state.shape
    ens = lax.axis_size("ens")
    members = mem * ens
    observed = obs_values.shape[1]
    width = FSTEPS
    f32 = functools.partial(jax.ShapeDtypeStruct, dtype=jnp.float32)
    scratch = functools.partial(pltpu.VMEM, dtype=jnp.float32)
    place = lax.axis_index("dom").astype(jnp.int32).reshape(1)
    staged = jnp.pad(state, ((0, 1), (0, 0), (0, 0))).reshape(-1, cols)
    def around(part):
        slots = [part] * ens
        for j in range(1, ens // 2 + 1):
            slots[j] = shift(slots[j - 1], "ens", 1)
        for j in range(1, (ens - 1) // 2 + 1):
            slots[ens - j] = shift(slots[(ens - j + 1) % ens], "ens", -1)
        return slots

    edge = f32((width, mem + 8, cols))
    cells, own = pl.pallas_call(
        rows_kernel,
        out_shape=(jax.ShapeDtypeStruct((8, observed), jnp.int32), f32((16, observed))),
        in_specs=[SMEM] * 2 + [VMEM] * 3,
        out_specs=(VMEM, VMEM),
        compiler_params=PARAMS,
        cost_estimate=estimate(1),
        name="rows",
    )(place, owners, obs_offsets, obs_values, obs_variance)
    inner, mixers = pl.pallas_call(
        inner_kernel,
        out_shape=(f32((rows - 2 * width, mem, cols)), f32((4, rows, cols))),
        in_specs=[VMEM] * 4,
        out_specs=(VMEM,) * 2,
        scratch_shapes=[scratch((rows, mem, cols))] * 2,
        compiler_params=PARAMS,
        cost_estimate=estimate(3),
        name="inner",
    )(staged, row_courant, col_courant, diffusion)
    top, upper, lower, bottom = pl.pallas_call(
        border_kernel,
        out_shape=(edge,) * 4,
        in_specs=[VMEM] * 2,
        out_specs=(VMEM,) * 4,
        compiler_params=PARAMS,
        cost_estimate=estimate(0.2),
        name="border",
    )(staged, mixers)
    up = shift(bottom, "dom", 1)
    down = shift(top, "dom", -1)
    outer, seen = pl.pallas_call(
        outer_kernel,
        out_shape=(f32((2 * width, mem, cols)), f32((mem, observed))),
        in_specs=[VMEM] * 8,
        out_specs=(VMEM, VMEM),
        scratch_shapes=[scratch((3 * width, mem, cols))] * 2,
        compiler_params=PARAMS,
        cost_estimate=estimate(2),
        name="outer",
    )(cells, up, top, upper, lower, bottom, down, inner)

    seens = [seen] + [shift(seen, "ens", k) for k in range(1, ens)]
    gram = pl.pallas_call(
        gram_kernel,
        out_shape=f32((members + 8, members)),
        in_specs=[VMEM] * (1 + ens),
        out_specs=VMEM,
        compiler_params=PARAMS,
        cost_estimate=estimate(1),
        name="gram",
    )(own, *seens)
    grams = lax.all_gather(gram, "dom")

    slots = list(zip(around(inner), around(outer)))
    late = list(range(2, ens - 1))
    soon = [j for j in range(ens) if j not in late]

    mix_soon, mix_late = pl.pallas_call(
        functools.partial(chain_kernel, soon, late),
        out_shape=(f32((mem, mem * len(soon))), f32((mem, mem * len(late)))),
        in_specs=[SMEM, VMEM],
        out_specs=(VMEM, VMEM),
        compiler_params=PARAMS,
        cost_estimate=estimate(CHAIN_US),
        name="chain",
    )(owners, grams)
    sums = pl.pallas_call(
        early_kernel,
        out_shape=f32((rows // 2, mem, 2 * cols)),
        in_specs=[VMEM] * (1 + 2 * len(soon)),
        out_specs=VMEM,
        compiler_params=PARAMS,
        cost_estimate=estimate(EARLY_US),
        name="early",
    )(mix_soon, *[x for j in soon for x in slots[j]])
    blocks = list(range(0, rows, 8))
    out = None
    for chosen, width_of in ((blocks[1:-1], 1), ((blocks[0], blocks[-1]), 2)):
        given = [x for j in late for x in slots[j][:width_of]]
        previous = [] if out is None else [out]
        out = pl.pallas_call(
            functools.partial(late_kernel, chosen, width_of),
            out_shape=f32((mem, rows, cols)),
            in_specs=[VMEM] * (2 + len(given)) + [ANY] * len(previous),
            out_specs=ANY,
            input_output_aliases={2 + len(given): 0} if previous else {},
            scratch_shapes=[scratch((mem, rows, cols)), pltpu.SemaphoreType.DMA((len(chosen),))],
            compiler_params=PARAMS,
            cost_estimate=estimate(0.1),
            name="late",
        )(mix_late, sums, *given, *previous)
    return out


def solution(mesh):
    return jax.shard_map(
        on_device,
        mesh=mesh,
        in_specs=(
            P("ens", "dom", None),
            P("dom", None),
            P("dom", None),
            P("dom", None),
            P(),
            P(),
            P(),
            P(),
        ),
        out_specs=P("ens", "dom", None),
        check_vma=False,
    )
```
